32 devices in a mesh: parts: 2 (over y), src: 4 (over x, core), space: 4 (over z).
Axes of the slice: x: 2, y: 2, z: 4, core: 2. Of those that a mesh axis runs over, the one named last changes fastest.
Arguments:
- fields: float32 [8, 4, 16, 128, 128], P(('parts', 'src'), None, 'space'), parts along dimension 0, may hold values from -6 to 6
- velocity: float32 [32, 128, 128], P(('parts', 'space')), parts along dimension 0, may hold values from 0.5 to 1
- conductivity: float32 [32, 128, 128], P(('parts', 'space')), parts along dimension 0, may hold values from 1 to 4
- labels: int32 [8], P(('parts', 'src')), parts along dimension 0, may hold values from 0 to 1, as said below
Outputs:
- fields_out: float32 [8, 2, 16, 128, 128], P(('parts', 'src'), None, 'space'), parts along dimension 0
- models_out: float32 [2, 32, 128, 128], P(None, ('parts', 'space')), parts along dimension 1
The draws below stay inside these ranges and needn't reach their ends.
There are 2 independent parts, one for each index of `parts`. The reference program is written for one: setup_inputs(seed, part) draws one part's arguments, and reference() takes and returns one part's arrays. A program takes and returns all parts, laid end to end along the dimension named above; each array names one. Nothing has to cross between parts.
Inputs may be any that keep to these rules, and one draw needn't show every extreme that they name: `labels`: at least one group has label 0 and at least one has label 1; the rest are drawn.
All inputs are finite; a program needn't handle non-finite values.
Results may differ from the reference program's by a relative error of at most 0.00002.
Values sent between devices are 32-bit elements; how exact they have to be, the bound alone decides.
A program may use at most 64 MiB of HBM per device.

```python
import math
import jax
import jax.numpy as jnp
from jax import lax

NY = 128
NZ = 128
STEPS = 3
G = 4
NX = 16


def draw_labels(key, part):
    key_bits = jax.random.fold_in(key, 11)
    key_zero = jax.random.fold_in(key, 23)
    key_one = jax.random.fold_in(key, 37)
    bits = jax.random.randint(key_bits, (G,), 0, 2).astype(jnp.int32)
    zero_pos = jax.random.randint(key_zero, (), 0, G).astype(jnp.int32)
    step_one = jax.random.randint(key_one, (), 1, G).astype(jnp.int32)
    one_pos = ((zero_pos + step_one) % G).astype(jnp.int32)
    bits = bits.at[zero_pos].set(0).at[one_pos].set(1)
    return bits.astype(jnp.int32)


def block_levels(stream_key, extent, cuts, smallest, largest):
    factor_of, own = 1.0, jax.random.fold_in(stream_key, 6)
    for dim, parts in cuts:
        draws = jnp.exp(jax.random.uniform(jax.random.fold_in(own, dim), (parts,), jnp.float32, smallest / len(cuts), largest / len(cuts)))
        factor_of = factor_of * jnp.repeat(draws, extent[dim] // parts).reshape([-1 if axis == dim else 1 for axis in range(len(extent))])
    return factor_of


def noise(rng, dims, width, most, split=(), dtype=jnp.bfloat16):
    values = jax.random.normal(rng, dims, jnp.float32) * width
    if len(split) > 0:
        values = block_levels(rng, dims, split, -0.22, 0.18) * values
    return jnp.clip(values, min=-most, max=most).astype(dtype)


def setup_inputs(seed: int = 0, part: int = 0) -> dict:
    seeds = jax.random.split(jax.random.key(seed), 5)
    own_keys = jax.random.split(jax.random.fold_in(seeds[4], part), 5)
    fields = noise(own_keys[0], (G, 4, NX, NY, NZ), 1.0, 6.0, ((0, 4), (2, 4)), jnp.float32)
    velocity = jnp.clip(0.5 + 0.5 * jax.random.uniform(own_keys[1], (NX, NY, NZ), jnp.float32) ** block_levels(own_keys[1], (NX, NY, NZ), ((0, 4),), -0.2, 0.2), 0.5, 1.0)
    conductivity = jnp.clip(jnp.exp(math.log(4.0) - 1.3862944 * jax.random.uniform(own_keys[2], (NX, NY, NZ), jnp.float32) ** block_levels(own_keys[2], (NX, NY, NZ), ((0, 4),), -0.2, 0.2)), 1.0, 4.0)
    labels = draw_labels(jax.random.fold_in(jax.random.fold_in(seeds[4], part), 71), part)
    return dict(fields=fields, velocity=velocity, conductivity=conductivity, labels=labels)


speed_gain = 0.25
diffuse_gain = 0.15
step_size = 0.1
penalty_gain = 50.0

def laplace(field):
    padded = jnp.pad(field, 1)
    total = padded[2:, 1:-1, 1:-1] + padded[:-2, 1:-1, 1:-1]
    total = total + padded[1:-1, 2:, 1:-1] + padded[1:-1, :-2, 1:-1]
    total = total + padded[1:-1, 1:-1, 2:] + padded[1:-1, 1:-1, :-2]
    return total - 6.0 * field

def coefficient(weight, velocity, conductivity):
    return weight * speed_gain * velocity ** 2 + (1.0 - weight) * diffuse_gain / conductivity

def advance(state, coef, weight):
    upper, upper_prev, lower, lower_prev = state
    accum = jnp.zeros_like(upper)
    for step in range(STEPS):
        lap_upper = laplace(upper)
        lap_lower = laplace(lower)
        accum = accum + lower * lap_upper
        upper_next = weight * (2.0 * upper - upper_prev) + (1.0 - weight) * upper + coef * lap_upper
        lower_next = weight * (2.0 * lower - lower_prev) + (1.0 - weight) * lower + coef * lap_lower
        upper_prev, upper = (upper, upper_next)
        lower_prev, lower = (lower, lower_next)
    return ((upper, upper_prev, lower, lower_prev), accum)

def centred(model):
    padded = jnp.pad(model, 1, mode='edge')
    along_x = (padded[2:, 1:-1, 1:-1] - padded[:-2, 1:-1, 1:-1]) * 0.5
    along_y = (padded[1:-1, 2:, 1:-1] - padded[1:-1, :-2, 1:-1]) * 0.5
    along_z = (padded[1:-1, 1:-1, 2:] - padded[1:-1, 1:-1, :-2]) * 0.5
    return (along_x, along_y, along_z)

def reference(fields, velocity, conductivity, labels):
    weights = labels.astype(jnp.float32)

    def first(item):
        group, weight = item
        coef = coefficient(weight, velocity, conductivity)
        state, accum = advance((group[0], group[1], group[2], group[3]), coef, weight)
        return (jnp.stack(state, 0), accum)
    states, accums = lax.map(first, (fields, weights))
    scale = 1.0 / (20.0 * jnp.sqrt(jnp.float32(G)))
    wide = weights[:, None, None, None]
    grad_v = scale * lax.optimization_barrier(jnp.sum(wide * accums, 0))
    grad_c = scale * lax.optimization_barrier(jnp.sum((1.0 - wide) * accums, 0))
    vx, vy, vz = centred(velocity)
    lx, ly, lz = centred(jnp.log(conductivity))
    cross_a = vy * lz - vz * ly
    cross_b = vz * lx - vx * lz
    cross_c = vx * ly - vy * lx
    penalty = penalty_gain * (cross_a * cross_a + cross_b * cross_b + cross_c * cross_c)
    new_velocity = velocity * jnp.exp(-step_size * jnp.tanh(grad_v + penalty))
    new_conductivity = conductivity * jnp.exp(-step_size * jnp.tanh(grad_c + penalty))

    def second(item):
        state, weight = item
        coef = coefficient(weight, new_velocity, new_conductivity)
        final, unused = advance((state[0], state[1], state[2], state[3]), coef, weight)
        return jnp.stack([final[0], final[2]], 0)
    fields_out = lax.map(second, (states, weights))
    return (fields_out, jnp.stack([new_velocity, new_conductivity], 0))
```

```python
import functools
import math

import jax
import jax.numpy as jnp
from jax import lax
from jax.experimental import pallas as pl
from jax.experimental.pallas import tpu as pltpu
from jax.sharding import PartitionSpec as P

STEPS = 3
PAD = 8
MESH = pl.DeviceIdType.MESH

speed_gain = 0.25
diffuse_gain = 0.15
step_size = 0.1
penalty_gain = 50.0


def coefficient(weight, velocity, conductivity):
    return weight * speed_gain * velocity**2 + (1.0 - weight) * diffuse_gain / conductivity


def kernel(
    spaces, srcs, groups,
    fields, velocity, conductivity, labels,
    fields_out, models_out,
    state, prev, halo, models, near, window, pen, coef, acc, got, label_own, label_got, fresh, updated, final,
    load_sem, model_sem, out_sem,
    halo_send, halo_recv, near_send, near_recv,
    label_send, label_recv, grad_send, grad_recv, fresh_send, fresh_recv,
):
    planes, ny, nz = fields.shape[2:]
    band = ny // srcs
    rows = 32 if ny % 32 == 0 else 8
    last = 2 * STEPS
    tile = lax.axis_index("space")
    me = lax.axis_index("src")
    offset = pl.multiple_of(me * band, 8)
    has_low = tile > 0
    has_high = tile < spaces - 1
    sides = ((has_low, tile - 1), (has_high, tile + 1))
    peers = [lax.rem(me + d, srcs) for d in range(1, srcs)]
    inner = list(range(1, planes - 1))
    edge = [0, planes - 1]
    slot = {p: p - 1 for p in inner}
    slot[0] = planes - 2
    slot[planes - 1] = planes - 1
    parts = ((0, planes - 2), (planes - 2, 2))

    loads = []
    for f in range(2):
        loads.append(pltpu.make_async_copy(
            fields.at[0, 2 * f], state.at[0, f, :, pl.ds(PAD, ny), :], load_sem.at[2 * f]))
        loads.append(pltpu.make_async_copy(fields.at[0, 2 * f + 1], prev.at[f], load_sem.at[2 * f + 1]))
    model_loads = [
        pltpu.make_async_copy(ref, models.at[m, :, pl.ds(PAD, ny), :], model_sem.at[m])
        for m, ref in enumerate((velocity, conductivity))
    ]
    for copy in loads + model_loads:
        copy.start()

    barrier = pltpu.get_barrier_semaphore()
    for exists, other in sides:
        @pl.when(exists)
        def _():
            pl.semaphore_signal(barrier, inc=1, device_id={"space": other}, device_id_type=MESH)
    for peer in peers:
        pl.semaphore_signal(barrier, inc=1, device_id={"src": peer}, device_id_type=MESH)

    weight = labels[0].astype(jnp.float32)
    label_own[...] = jnp.full(label_own.shape, weight, jnp.float32)
    lane = lax.broadcasted_iota(jnp.int32, (1, nz), 1)
    first_lane = lane == 0
    last_lane = lane == nz - 1
    zero_rows = jnp.zeros((PAD, nz), jnp.float32)
    for k in range(last):
        for f in range(2):
            for p in range(planes):
                state[k, f, p, pl.ds(0, PAD), :] = zero_rows
                state[k, f, p, pl.ds(PAD + ny, PAD), :] = zero_rows

    pl.semaphore_wait(barrier, srcs - 1 + has_low.astype(jnp.int32) + has_high.astype(jnp.int32))

    def halo_copy(k, f, side):
        plane = 0 if side == 0 else planes - 1
        if k == 0:
            source = fields.at[0, 2 * f, plane]
        else:
            source = state.at[k, f, plane, pl.ds(PAD, ny), :]
        return pltpu.make_async_remote_copy(
            src_ref=source, dst_ref=halo.at[k, f, 1 - side],
            send_sem=halo_send.at[k, f, side], recv_sem=halo_recv.at[k, f, 1 - side],
            device_id={"space": sides[side][1]}, device_id_type=MESH)

    def halo_start(k, f):
        for side in range(2):
            @pl.when(sides[side][0])
            def _():
                halo_copy(k, f, side).start()

    def halo_wait(k, f, side):
        @pl.when(sides[side][0])
        def _():
            pltpu.make_async_remote_copy(
                src_ref=halo.at[k, f, side], dst_ref=halo.at[k, f, side],
                send_sem=halo_send.at[k, f, side], recv_sem=halo_recv.at[k, f, side],
                device_id={"space": sides[side][1]}, device_id_type=MESH).wait_recv()

    def near_copy(m, side):
        ref = (velocity, conductivity)[m]
        plane = 0 if side == 0 else planes - 1
        return pltpu.make_async_remote_copy(
            src_ref=ref.at[plane, pl.ds(offset, band), :], dst_ref=near.at[m, 1 - side],
            send_sem=near_send.at[m, side], recv_sem=near_recv.at[m, 1 - side],
            device_id={"space": sides[side][1]}, device_id_type=MESH)

    def near_wait(m, side):
        pltpu.make_async_remote_copy(
            src_ref=near.at[m, side], dst_ref=near.at[m, side],
            send_sem=near_send.at[m, side], recv_sem=near_recv.at[m, side],
            device_id={"space": sides[side][1]}, device_id_type=MESH).wait_recv()

    def label_copy(d):
        return pltpu.make_async_remote_copy(
            src_ref=label_own, dst_ref=label_got.at[d],
            send_sem=label_send.at[d], recv_sem=label_recv.at[d],
            device_id={"src": peers[d]}, device_id_type=MESH)

    def grad_copy(part, d):
        begin, count = parts[part]
        return pltpu.make_async_remote_copy(
            src_ref=acc.at[pl.ds(begin, count), pl.ds(pl.multiple_of(peers[d] * band, 8), band), :],
            dst_ref=got.at[d, pl.ds(begin, count)],
            send_sem=grad_send.at[part, d], recv_sem=grad_recv.at[part, d],
            device_id={"src": peers[d]}, device_id_type=MESH)

    def fresh_copy(part, d):
        begin, count = parts[part]
        return pltpu.make_async_remote_copy(
            src_ref=fresh.at[:, pl.ds(begin, count)],
            dst_ref=updated.at[:, pl.ds(begin, count), pl.ds(offset, band), :],
            send_sem=fresh_send.at[part, d], recv_sem=fresh_recv.at[part, d],
            device_id={"src": peers[d]}, device_id_type=MESH)

    def fresh_wait(part, d):
        begin, count = parts[part]
        source = pl.multiple_of(lax.rem(me + srcs - 1 - d, srcs) * band, 8)
        ref = updated.at[:, pl.ds(begin, count), pl.ds(source, band), :]
        pltpu.make_async_remote_copy(
            src_ref=ref, dst_ref=ref,
            send_sem=fresh_send.at[part, d], recv_sem=fresh_recv.at[part, d],
            device_id={"src": peers[d]}, device_id_type=MESH).wait_recv()

    halo_start(0, 0)
    halo_start(0, 1)
    for side in range(2):
        @pl.when(sides[side][0])
        def _():
            for m in range(2):
                near_copy(m, side).start()
    for d in range(srcs - 1):
        label_copy(d).start()

    for side in range(2):
        @pl.when(jnp.logical_not(sides[side][0]))
        def _():
            for k in range(last):
                for f in range(2):
                    halo[k, f, side] = jnp.zeros((ny, nz), jnp.float32)

    def in_rows(body):
        def step(i, carry):
            body(pl.multiple_of(i * rows, 8))
            return carry
        lax.fori_loop(0, ny // rows, step, 0, unroll=True)

    keep_gain = 1.0 + weight

    def advance(k, f, p):
        def body(r):
            def at(plane, shift):
                return state[k, f, plane, pl.ds(r + PAD + shift, rows), :]
            middle = at(p, 0)
            below = halo[k, f, 0, pl.ds(r, rows), :] if p == 0 else at(p - 1, 0)
            above = halo[k, f, 1, pl.ds(r, rows), :] if p == planes - 1 else at(p + 1, 0)
            total = below + above
            total = total + at(p, 1) + at(p, -1)
            right = jnp.where(last_lane, 0.0, pltpu.roll(middle, nz - 1, 1))
            left = jnp.where(first_lane, 0.0, pltpu.roll(middle, 1, 1))
            lap = total + right + left - 6.0 * middle
            if f == 0 and k < STEPS:
                term = state[k, 1, p, pl.ds(r + PAD, rows), :] * lap
                if k == 0:
                    acc[slot[p], pl.ds(r, rows), :] = term
                else:
                    acc[slot[p], pl.ds(r, rows), :] += term
            if k == 0:
                before = prev[f, p, pl.ds(r, rows), :]
            else:
                before = state[k - 1, f, p, pl.ds(r + PAD, rows), :]
            value = keep_gain * middle - weight * before + coef[slot[p], pl.ds(r, rows), :] * lap
            if k == last - 1:
                final[f, p, pl.ds(r, rows), :] = value
            else:
                state[k + 1, f, p, pl.ds(r + PAD, rows), :] = value
        in_rows(body)

    def out_copy(f, p):
        return pltpu.make_async_copy(final.at[f, p], fields_out.at[0, f, p], out_sem.at[f, p])

    def model_out_copy(m, p):
        return pltpu.make_async_copy(updated.at[m, slot[p]], models_out.at[m, p], out_sem.at[2 + m, p])

    def form_coef(p, velocity_at, conductivity_at):
        def body(r):
            coef[slot[p], pl.ds(r, rows), :] = coefficient(weight, velocity_at(p, r), conductivity_at(p, r))
        in_rows(body)

    for copy in model_loads:
        copy.wait()
    for p in range(planes):
        form_coef(
            p,
            lambda p, r: models[0, p, pl.ds(r + PAD, rows), :],
            lambda p, r: models[1, p, pl.ds(r + PAD, rows), :],
        )
        for m in range(2):
            models[m, p, pl.ds(0, PAD), :] = jnp.broadcast_to(models[m, p, pl.ds(PAD, 1), :], (PAD, nz))
            models[m, p, pl.ds(PAD + ny, PAD), :] = jnp.broadcast_to(
                models[m, p, pl.ds(PAD + ny - 1, 1), :], (PAD, nz))
    for copy in loads:
        copy.wait()

    def boundary(k, f):
        for side in range(2):
            halo_wait(k, f, side)
            advance(k, f, edge[side])
            if k + 1 < last:
                @pl.when(sides[side][0])
                def _():
                    halo_copy(k + 1, f, side).start()
            else:
                out_copy(f, edge[side]).start()

    def interior(k, f):
        for p in inner:
            advance(k, f, p)
            if k == last - 1:
                out_copy(f, p).start()

    def penalty():
        def prepare(p, carry):
            window[0, p] = models[0, p, pl.ds(offset, band + 2 * PAD), :]
            window[1, p] = jnp.log(models[1, p, pl.ds(offset, band + 2 * PAD), :])
            return carry
        for p in range(planes):
            prepare(p, 0)
        for side in range(2):
            @pl.when(sides[side][0])
            def _():
                for m in range(2):
                    near_wait(m, side)
                near[1, side] = jnp.log(near[1, side])

            @pl.when(jnp.logical_not(sides[side][0]))
            def _():
                for m in range(2):
                    near[m, side] = window[m, edge[side], pl.ds(PAD, band), :]
        for p in range(planes):
            diffs = []
            for m in range(2):
                middle = window[m, p, pl.ds(PAD, band), :]
                below = near[m, 0] if p == 0 else window[m, p - 1, pl.ds(PAD, band), :]
                above = near[m, 1] if p == planes - 1 else window[m, p + 1, pl.ds(PAD, band), :]
                dx = (above - below) * 0.5
                dy = (window[m, p, pl.ds(PAD + 1, band), :] - window[m, p, pl.ds(PAD - 1, band), :]) * 0.5
                right = jnp.where(last_lane, middle, pltpu.roll(middle, nz - 1, 1))
                left = jnp.where(first_lane, middle, pltpu.roll(middle, 1, 1))
                diffs.append((dx, dy, (right - left) * 0.5))
            (vx, vy, vz), (lx, ly, lz) = diffs
            cross_a = vy * lz - vz * ly
            cross_b = vz * lx - vx * lz
            cross_c = vx * ly - vy * lx
            pen[slot[p]] = penalty_gain * (cross_a * cross_a + cross_b * cross_b + cross_c * cross_c)

    scale = 1.0 / (20.0 * math.sqrt(groups))

    def renew(part):
        for d in range(srcs - 1):
            if part == 0:
                label_copy(d).wait_recv()
            grad_copy(part, d).wait_recv()
        begin, count = parts[part]
        for s in range(begin, begin + count):
            p = [q for q in slot if slot[q] == s][0]
            own = acc[s, pl.ds(offset, band), :]
            grad_v = weight * own
            grad_c = (1.0 - weight) * own
            for d in range(srcs - 1):
                theirs = got[d, s]
                label = label_got[d, pl.ds(0, 1), :]
                grad_v = grad_v + label * theirs
                grad_c = grad_c + (1.0 - label) * theirs
            for m, grad in enumerate((grad_v, grad_c)):
                old = models[m, p, pl.ds(offset + PAD, band), :]
                value = old * jnp.exp(-step_size * jnp.tanh(scale * grad + pen[s]))
                fresh[m, s] = value
                updated[m, s, pl.ds(offset, band), :] = value
        for d in range(srcs - 1):
            fresh_copy(part, d).start()

    def take_models(part, chosen):
        for d in range(srcs - 1):
            fresh_wait(part, d)
        for p in chosen:
            form_coef(
                p,
                lambda p, r: updated[0, slot[p], pl.ds(r, rows), :],
                lambda p, r: updated[1, slot[p], pl.ds(r, rows), :],
            )

    for k in range(STEPS):
        interior(k, 0)
        if k == STEPS - 1:
            for d in range(srcs - 1):
                grad_copy(0, d).start()
        interior(k, 1)
        if k == 1:
            penalty()
        boundary(k, 0)
        if k == STEPS - 1:
            for d in range(srcs - 1):
                grad_copy(1, d).start()
        boundary(k, 1)

    renew(0)
    renew(1)
    take_models(0, inner)
    interior(STEPS, 0)
    interior(STEPS, 1)
    take_models(1, edge)
    boundary(STEPS, 0)
    boundary(STEPS, 1)
    for m in range(2):
        for p in range(planes):
            model_out_copy(m, p).start()
    for k in range(STEPS + 1, last):
        interior(k, 0)
        interior(k, 1)
        boundary(k, 0)
        boundary(k, 1)

    for side in range(2):
        @pl.when(sides[side][0])
        def _():
            for m in range(2):
                near_copy(m, side).wait_send()
            for k in range(last):
                for f in range(2):
                    halo_copy(k, f, side).wait_send()
    for d in range(srcs - 1):
        label_copy(d).wait_send()
        for part in range(2):
            grad_copy(part, d).wait_send()
            fresh_copy(part, d).wait_send()
    for p in range(planes):
        for f in range(2):
            out_copy(f, p).wait()
            model_out_copy(f, p).wait()


def shards(spaces, srcs, fields, velocity, conductivity, labels):
    planes, ny, nz = fields.shape[2:]
    band = ny // srcs
    last = 2 * STEPS
    groups = labels.shape[0] * srcs
    f32 = jnp.float32
    vmem = lambda *shape: pltpu.VMEM(shape, f32)
    dma = lambda *shape: pltpu.SemaphoreType.DMA(shape)
    anywhere = pl.BlockSpec(memory_space=pl.ANY)
    scratch = [
        vmem(last, 2, planes, ny + 2 * PAD, nz),
        vmem(2, planes, ny, nz),
        vmem(last, 2, 2, ny, nz),
        vmem(2, planes, ny + 2 * PAD, nz),
        vmem(2, 2, band, nz),
        vmem(2, planes, band + 2 * PAD, nz),
        vmem(planes, band, nz),
        vmem(planes, ny, nz),
        vmem(planes, ny, nz),
        vmem(srcs - 1, planes, band, nz),
        vmem(8, nz),
        vmem(srcs - 1, 8, nz),
        vmem(2, planes, band, nz),
        vmem(2, planes, ny, nz),
        vmem(2, planes, ny, nz),
        dma(4), dma(2), dma(4, planes),
        dma(last, 2, 2), dma(last, 2, 2), dma(2, 2), dma(2, 2),
        dma(srcs - 1), dma(srcs - 1), dma(2, srcs - 1), dma(2, srcs - 1), dma(2, srcs - 1), dma(2, srcs - 1),
    ]
    return tuple(pl.pallas_call(
        functools.partial(kernel, spaces, srcs, groups),
        out_shape=(
            jax.ShapeDtypeStruct((1, 2, planes, ny, nz), f32),
            jax.ShapeDtypeStruct((2, planes, ny, nz), f32),
        ),
        in_specs=[anywhere] * 3 + [pl.BlockSpec(memory_space=pltpu.SMEM)],
        out_specs=(anywhere, anywhere),
        scratch_shapes=scratch,
        cost_estimate=pl.CostEstimate(
            flops=40 * last * 2 * planes * ny * nz, bytes_accessed=40 * planes * ny * nz, transcendentals=0),
        compiler_params=pltpu.CompilerParams(
            collective_id=0, has_side_effects=True, vmem_limit_bytes=32 * 1024 * 1024),
    )(fields, velocity, conductivity, labels))


def solution(mesh):
    in_specs = (
        P(("parts", "src"), None, "space", None, None),
        P(("parts", "space"), None, None),
        P(("parts", "space"), None, None),
        P(("parts", "src")),
    )
    out_specs = (
        P(("parts", "src"), None, "space", None, None),
        P(None, ("parts", "space"), None, None),
    )
    body = functools.partial(shards, mesh.shape["space"], mesh.shape["src"])
    return jax.shard_map(body, mesh=mesh, in_specs=in_specs, out_specs=out_specs, check_vma=False)
```

```python
import functools
import math

import jax
import jax.numpy as jnp
from jax import lax
from jax.experimental import pallas as pl
from jax.experimental.pallas import tpu as pltpu
from jax.sharding import PartitionSpec as P

STEPS = 3
PAD = 8
MESH = pl.DeviceIdType.MESH

speed_gain = 0.25
diffuse_gain = 0.15
step_size = 0.1
penalty_gain = 50.0


def coefficient(weight, velocity, conductivity):
    return weight * speed_gain * velocity**2 + (1.0 - weight) * diffuse_gain / conductivity


def kernel(
    spaces, srcs, groups,
    fields, velocity, conductivity, labels,
    fields_out, models_out,
    state, prev, halo, models, near, window, pen, coef, acc, got, label_own, label_got, fresh, updated, ordered, final,
    load_sem, model_sem, out_sem,
    halo_send, halo_recv, near_send, near_recv,
    label_send, label_recv, grad_send, grad_recv, fresh_send, fresh_recv,
):
    planes, ny, nz = fields.shape[2:]
    band = ny // srcs
    rows = 32 if ny % 32 == 0 else 8
    last = 2 * STEPS
    tile = lax.axis_index("space")
    me = lax.axis_index("src")
    offset = pl.multiple_of(me * band, 8)
    has_low = tile > 0
    has_high = tile < spaces - 1
    sides = ((has_low, tile - 1), (has_high, tile + 1))
    peers = [lax.rem(me + d, srcs) for d in range(1, srcs)]
    inner = list(range(1, planes - 1))
    edge = [0, planes - 1]
    slot = {p: p - 1 for p in inner}
    slot[0] = planes - 2
    slot[planes - 1] = planes - 1
    parts = ((0, planes - 2), (planes - 2, 1), (planes - 1, 1))

    loads = []
    for f in range(2):
        loads.append(pltpu.make_async_copy(
            fields.at[0, 2 * f], state.at[0, f, :, pl.ds(PAD, ny), :], load_sem.at[2 * f]))
        loads.append(pltpu.make_async_copy(fields.at[0, 2 * f + 1], prev.at[f], load_sem.at[2 * f + 1]))
    model_loads = [
        pltpu.make_async_copy(ref, models.at[m, :, pl.ds(PAD, ny), :], model_sem.at[m])
        for m, ref in enumerate((velocity, conductivity))
    ]
    for copy in loads + model_loads:
        copy.start()

    barrier = pltpu.get_barrier_semaphore()
    for exists, other in sides:
        @pl.when(exists)
        def _():
            pl.semaphore_signal(barrier, inc=1, device_id={"space": other}, device_id_type=MESH)
    for peer in peers:
        pl.semaphore_signal(barrier, inc=1, device_id={"src": peer}, device_id_type=MESH)

    weight = labels[0].astype(jnp.float32)
    label_own[...] = jnp.full(label_own.shape, weight, jnp.float32)
    lane = lax.broadcasted_iota(jnp.int32, (1, nz), 1)
    first_lane = lane == 0
    last_lane = lane == nz - 1
    zero_rows = jnp.zeros((PAD, nz), jnp.float32)
    for k in range(last):
        for f in range(2):
            for p in range(planes):
                state[k, f, p, pl.ds(0, PAD), :] = zero_rows
                state[k, f, p, pl.ds(PAD + ny, PAD), :] = zero_rows

    pl.semaphore_wait(barrier, srcs - 1 + has_low.astype(jnp.int32) + has_high.astype(jnp.int32))

    def halo_copy(k, f, side):
        plane = 0 if side == 0 else planes - 1
        if k == 0:
            source = fields.at[0, 2 * f, plane]
        else:
            source = state.at[k, f, plane, pl.ds(PAD, ny), :]
        return pltpu.make_async_remote_copy(
            src_ref=source, dst_ref=halo.at[k, f, 1 - side],
            send_sem=halo_send.at[k, f, side], recv_sem=halo_recv.at[k, f, 1 - side],
            device_id={"space": sides[side][1]}, device_id_type=MESH)

    def halo_start(k, f):
        for side in range(2):
            @pl.when(sides[side][0])
            def _():
                halo_copy(k, f, side).start()

    def halo_wait(k, f, side):
        @pl.when(sides[side][0])
        def _():
            pltpu.make_async_remote_copy(
                src_ref=halo.at[k, f, side], dst_ref=halo.at[k, f, side],
                send_sem=halo_send.at[k, f, side], recv_sem=halo_recv.at[k, f, side],
                device_id={"space": sides[side][1]}, device_id_type=MESH).wait_recv()

    def near_copy(m, side):
        ref = (velocity, conductivity)[m]
        plane = 0 if side == 0 else planes - 1
        return pltpu.make_async_remote_copy(
            src_ref=ref.at[plane, pl.ds(offset, band), :], dst_ref=near.at[m, 1 - side],
            send_sem=near_send.at[m, side], recv_sem=near_recv.at[m, 1 - side],
            device_id={"space": sides[side][1]}, device_id_type=MESH)

    def near_wait(m, side):
        pltpu.make_async_remote_copy(
            src_ref=near.at[m, side], dst_ref=near.at[m, side],
            send_sem=near_send.at[m, side], recv_sem=near_recv.at[m, side],
            device_id={"space": sides[side][1]}, device_id_type=MESH).wait_recv()

    def label_copy(d):
        return pltpu.make_async_remote_copy(
            src_ref=label_own, dst_ref=label_got.at[d],
            send_sem=label_send.at[d], recv_sem=label_recv.at[d],
            device_id={"src": peers[d]}, device_id_type=MESH)

    def grad_copy(part, d):
        begin, count = parts[part]
        return pltpu.make_async_remote_copy(
            src_ref=acc.at[pl.ds(begin, count), pl.ds(pl.multiple_of(peers[d] * band, 8), band), :],
            dst_ref=got.at[d, pl.ds(begin, count)],
            send_sem=grad_send.at[part, d], recv_sem=grad_recv.at[part, d],
            device_id={"src": peers[d]}, device_id_type=MESH)

    def fresh_copy(kind, part, d):
        begin, count = parts[part]
        return pltpu.make_async_remote_copy(
            src_ref=fresh.at[kind, d, pl.ds(begin, count)],
            dst_ref=updated.at[kind, pl.ds(begin, count), pl.ds(offset, band), :],
            send_sem=fresh_send.at[kind, part, d], recv_sem=fresh_recv.at[kind, part, d],
            device_id={"src": peers[d]}, device_id_type=MESH)

    def fresh_wait(kind, part, d):
        begin, count = parts[part]
        source = pl.multiple_of(lax.rem(me + srcs - 1 - d, srcs) * band, 8)
        ref = updated.at[kind, pl.ds(begin, count), pl.ds(source, band), :]
        pltpu.make_async_remote_copy(
            src_ref=ref, dst_ref=ref,
            send_sem=fresh_send.at[kind, part, d], recv_sem=fresh_recv.at[kind, part, d],
            device_id={"src": peers[d]}, device_id_type=MESH).wait_recv()

    halo_start(0, 0)
    halo_start(0, 1)
    for side in range(2):
        @pl.when(sides[side][0])
        def _():
            for m in range(2):
                near_copy(m, side).start()
    for d in range(srcs - 1):
        label_copy(d).start()

    for side in range(2):
        @pl.when(jnp.logical_not(sides[side][0]))
        def _():
            for k in range(last):
                for f in range(2):
                    halo[k, f, side] = jnp.zeros((ny, nz), jnp.float32)

    def in_rows(body):
        def step(i, carry):
            body(pl.multiple_of(i * rows, 8))
            return carry
        lax.fori_loop(0, ny // rows, step, 0, unroll=True)

    keep_gain = 1.0 + weight

    def advance(k, f, p):
        def body(r):
            def at(plane, shift):
                return state[k, f, plane, pl.ds(r + PAD + shift, rows), :]
            middle = at(p, 0)
            below = halo[k, f, 0, pl.ds(r, rows), :] if p == 0 else at(p - 1, 0)
            above = halo[k, f, 1, pl.ds(r, rows), :] if p == planes - 1 else at(p + 1, 0)
            total = below + above
            total = total + at(p, 1) + at(p, -1)
            right = jnp.where(last_lane, 0.0, pltpu.roll(middle, nz - 1, 1))
            left = jnp.where(first_lane, 0.0, pltpu.roll(middle, 1, 1))
            lap = total + right + left - 6.0 * middle
            if f == 0 and k < STEPS:
                term = state[k, 1, p, pl.ds(r + PAD, rows), :] * lap
                if k == 0:
                    acc[slot[p], pl.ds(r, rows), :] = term
                else:
                    acc[slot[p], pl.ds(r, rows), :] += term
            if k == 0:
                before = prev[f, p, pl.ds(r, rows), :]
            else:
                before = state[k - 1, f, p, pl.ds(r + PAD, rows), :]
            value = keep_gain * middle - weight * before + coef[slot[p], pl.ds(r, rows), :] * lap
            if k == last - 1:
                final[f, p, pl.ds(r, rows), :] = value
            else:
                state[k + 1, f, p, pl.ds(r + PAD, rows), :] = value
        in_rows(body)

    def out_copy(f, p):
        return pltpu.make_async_copy(final.at[f, p], fields_out.at[0, f, p], out_sem.at[f, p])

    def model_out_copy(m, p):
        return pltpu.make_async_copy(ordered.at[m, p], models_out.at[m, p], out_sem.at[2 + m, p])

    def form_coef(p, velocity_at, conductivity_at):
        def body(r):
            coef[slot[p], pl.ds(r, rows), :] = coefficient(weight, velocity_at(p, r), conductivity_at(p, r))
        in_rows(body)

    for copy in model_loads:
        copy.wait()
    for p in range(planes):
        form_coef(
            p,
            lambda p, r: models[0, p, pl.ds(r + PAD, rows), :],
            lambda p, r: models[1, p, pl.ds(r + PAD, rows), :],
        )
        for m in range(2):
            models[m, p, pl.ds(0, PAD), :] = jnp.broadcast_to(models[m, p, pl.ds(PAD, 1), :], (PAD, nz))
            models[m, p, pl.ds(PAD + ny, PAD), :] = jnp.broadcast_to(
                models[m, p, pl.ds(PAD + ny - 1, 1), :], (PAD, nz))
    for copy in loads:
        copy.wait()

    def boundary(k, f, then=None):
        for side in range(2):
            halo_wait(k, f, side)
            advance(k, f, edge[side])
            if then is not None:
                then(side)
            if k + 1 < last:
                @pl.when(sides[side][0])
                def _():
                    halo_copy(k + 1, f, side).start()
            else:
                out_copy(f, edge[side]).start()

    def interior(k, f):
        for p in inner:
            advance(k, f, p)
            if k == last - 1:
                out_copy(f, p).start()

    def penalty():
        def prepare(p, carry):
            window[0, p] = models[0, p, pl.ds(offset, band + 2 * PAD), :]
            window[1, p] = jnp.log(models[1, p, pl.ds(offset, band + 2 * PAD), :])
            return carry
        for p in range(planes):
            prepare(p, 0)
        for side in range(2):
            @pl.when(sides[side][0])
            def _():
                for m in range(2):
                    near_wait(m, side)
                near[1, side] = jnp.log(near[1, side])

            @pl.when(jnp.logical_not(sides[side][0]))
            def _():
                for m in range(2):
                    near[m, side] = window[m, edge[side], pl.ds(PAD, band), :]
        for p in range(planes):
            diffs = []
            for m in range(2):
                middle = window[m, p, pl.ds(PAD, band), :]
                below = near[m, 0] if p == 0 else window[m, p - 1, pl.ds(PAD, band), :]
                above = near[m, 1] if p == planes - 1 else window[m, p + 1, pl.ds(PAD, band), :]
                dx = (above - below) * 0.5
                dy = (window[m, p, pl.ds(PAD + 1, band), :] - window[m, p, pl.ds(PAD - 1, band), :]) * 0.5
                right = jnp.where(last_lane, middle, pltpu.roll(middle, nz - 1, 1))
                left = jnp.where(first_lane, middle, pltpu.roll(middle, 1, 1))
                diffs.append((dx, dy, (right - left) * 0.5))
            (vx, vy, vz), (lx, ly, lz) = diffs
            cross_a = vy * lz - vz * ly
            cross_b = vz * lx - vx * lz
            cross_c = vx * ly - vy * lx
            pen[slot[p]] = penalty_gain * (cross_a * cross_a + cross_b * cross_b + cross_c * cross_c)

    scale = 1.0 / (20.0 * math.sqrt(groups))

    def renew(part):
        if part == 0:
            for d in range(srcs - 1):
                label_copy(d).wait_recv()
        for d in range(srcs - 1):
            grad_copy(part, d).wait_recv()
        begin, count = parts[part]
        for s in range(begin, begin + count):
            p = [q for q in slot if slot[q] == s][0]
            own = acc[s, pl.ds(offset, band), :]
            grad_v = weight * own
            grad_c = (1.0 - weight) * own
            for d in range(srcs - 1):
                theirs = got[d, s]
                label = label_got[d, pl.ds(0, 1), :]
                grad_v = grad_v + label * theirs
                grad_c = grad_c + (1.0 - label) * theirs
            new = []
            for m, grad in enumerate((grad_v, grad_c)):
                old = models[m, p, pl.ds(offset + PAD, band), :]
                new.append(old * jnp.exp(-step_size * jnp.tanh(scale * grad + pen[s])))
            for d in range(srcs):
                label = weight if d == srcs - 1 else label_got[srcs - 2 - d, pl.ds(0, 1), :]
                acoustic = jnp.broadcast_to(label, (band, nz)) > 0.5
                needed = jnp.where(acoustic, new[0], new[1])
                other = jnp.where(acoustic, new[1], new[0])
                if d == srcs - 1:
                    updated[0, s, pl.ds(offset, band), :] = needed
                    updated[1, s, pl.ds(offset, band), :] = other
                else:
                    fresh[0, d, s] = needed
                    fresh[1, d, s] = other
        for d in range(srcs - 1):
            fresh_copy(0, part, d).start()

    def take_models(part, chosen):
        for d in range(srcs - 1):
            fresh_wait(0, part, d)
        for p in chosen:
            form_coef(
                p,
                lambda p, r: updated[0, slot[p], pl.ds(r, rows), :],
                lambda p, r: updated[0, slot[p], pl.ds(r, rows), :],
            )

    def store_models():
        for part in range(3):
            for d in range(srcs - 1):
                fresh_wait(1, part, d)
        for p in range(planes):
            def body(r):
                needed = updated[0, slot[p], pl.ds(r, rows), :]
                other = updated[1, slot[p], pl.ds(r, rows), :]
                acoustic = jnp.full((rows, nz), weight) > 0.5
                ordered[0, p, pl.ds(r, rows), :] = jnp.where(acoustic, needed, other)
                ordered[1, p, pl.ds(r, rows), :] = jnp.where(acoustic, other, needed)
            in_rows(body)
            for m in range(2):
                model_out_copy(m, p).start()

    for k in range(STEPS - 1):
        interior(k, 0)
        interior(k, 1)
        if k == STEPS - 2:
            penalty()
        boundary(k, 0)
        boundary(k, 1)

    def send_grad(part):
        for d in range(srcs - 1):
            grad_copy(part, d).start()

    interior(STEPS - 1, 0)
    send_grad(0)
    interior(STEPS - 1, 1)
    boundary(STEPS - 1, 0, lambda side: send_grad(1 + side))
    renew(0)
    boundary(STEPS - 1, 1)
    renew(1)
    renew(2)
    take_models(0, inner)
    interior(STEPS, 0)
    interior(STEPS, 1)
    for side in range(2):
        take_models(1 + side, edge[side:side + 1])
    boundary(STEPS, 0)
    boundary(STEPS, 1)
    for part in range(3):
        for d in range(srcs - 1):
            fresh_copy(1, part, d).start()
    for k in range(STEPS + 1, last):
        interior(k, 0)
        interior(k, 1)
        if k == last - 1:
            store_models()
        boundary(k, 0)
        boundary(k, 1)

    for side in range(2):
        @pl.when(sides[side][0])
        def _():
            for m in range(2):
                near_copy(m, side).wait_send()
            for k in range(last):
                for f in range(2):
                    halo_copy(k, f, side).wait_send()
    for d in range(srcs - 1):
        label_copy(d).wait_send()
        for part in range(3):
            grad_copy(part, d).wait_send()
            for kind in range(2):
                fresh_copy(kind, part, d).wait_send()
    for p in range(planes):
        for f in range(2):
            out_copy(f, p).wait()
            model_out_copy(f, p).wait()


def shards(spaces, srcs, fields, velocity, conductivity, labels):
    planes, ny, nz = fields.shape[2:]
    band = ny // srcs
    last = 2 * STEPS
    groups = labels.shape[0] * srcs
    f32 = jnp.float32
    vmem = lambda *shape: pltpu.VMEM(shape, f32)
    dma = lambda *shape: pltpu.SemaphoreType.DMA(shape)
    anywhere = pl.BlockSpec(memory_space=pl.ANY)
    scratch = [
        vmem(last, 2, planes, ny + 2 * PAD, nz),
        vmem(2, planes, ny, nz),
        vmem(last, 2, 2, ny, nz),
        vmem(2, planes, ny + 2 * PAD, nz),
        vmem(2, 2, band, nz),
        vmem(2, planes, band + 2 * PAD, nz),
        vmem(planes, band, nz),
        vmem(planes, ny, nz),
        vmem(planes, ny, nz),
        vmem(srcs - 1, planes, band, nz),
        vmem(8, nz),
        vmem(srcs - 1, 8, nz),
        vmem(2, srcs - 1, planes, band, nz),
        vmem(2, planes, ny, nz),
        vmem(2, planes, ny, nz),
        vmem(2, planes, ny, nz),
        dma(4), dma(2), dma(4, planes),
        dma(last, 2, 2), dma(last, 2, 2), dma(2, 2), dma(2, 2),
        dma(srcs - 1), dma(srcs - 1), dma(3, srcs - 1), dma(3, srcs - 1),
        dma(2, 3, srcs - 1), dma(2, 3, srcs - 1),
    ]
    return tuple(pl.pallas_call(
        functools.partial(kernel, spaces, srcs, groups),
        out_shape=(
            jax.ShapeDtypeStruct((1, 2, planes, ny, nz), f32),
            jax.ShapeDtypeStruct((2, planes, ny, nz), f32),
        ),
        in_specs=[pl.BlockSpec(memory_space=pltpu.HBM)] * 3 + [pl.BlockSpec(memory_space=pltpu.SMEM)],
        out_specs=(anywhere, anywhere),
        scratch_shapes=scratch,
        cost_estimate=pl.CostEstimate(
            flops=40 * last * 2 * planes * ny * nz, bytes_accessed=40 * planes * ny * nz, transcendentals=0),
        compiler_params=pltpu.CompilerParams(
            collective_id=0, has_side_effects=True, vmem_limit_bytes=56 * 1024 * 1024),
    )(fields, velocity, conductivity, labels))


def solution(mesh):
    in_specs = (
        P(("parts", "src"), None, "space", None, None),
        P(("parts", "space"), None, None),
        P(("parts", "space"), None, None),
        P(("parts", "src")),
    )
    out_specs = (
        P(("parts", "src"), None, "space", None, None),
        P(None, ("parts", "space"), None, None),
    )
    body = functools.partial(shards, mesh.shape["space"], mesh.shape["src"])
    return jax.shard_map(body, mesh=mesh, in_specs=in_specs, out_specs=out_specs, check_vma=False)
```

```python
import functools
import math

import jax
import jax.numpy as jnp
from jax import lax
from jax.experimental import pallas as pl
from jax.experimental.pallas import tpu as pltpu
from jax.sharding import PartitionSpec as P

STEPS = 3
PAD = 8
PIECES = 2
MESH = pl.DeviceIdType.MESH

speed_gain = 0.25
diffuse_gain = 0.15
step_size = 0.1
penalty_gain = 50.0


def coefficient(weight, velocity, conductivity):
    return weight * speed_gain * velocity**2 + (1.0 - weight) * diffuse_gain / conductivity


def kernel(
    spaces, srcs, groups,
    fields, velocity, conductivity, labels,
    fields_out, models_out,
    state, prev, halo, models, near, window, pen, coef, acc, got, label_own, label_got, fresh, updated,
    load_sem, model_sem,
    halo_send, halo_recv, near_send, near_recv,
    label_send, label_recv, grad_send, grad_recv, fresh_send, fresh_recv,
):
    planes, ny, nz = fields.shape[2:]
    band = ny // srcs
    piece = ny // PIECES
    rows = 32 if piece % 32 == 0 else 8
    last = 2 * STEPS
    tile = lax.axis_index("space")
    me = lax.axis_index("src")
    offset = pl.multiple_of(me * band, 8)
    has_low = tile > 0
    has_high = tile < spaces - 1
    sides = ((has_low, tile - 1), (has_high, tile + 1))
    peers = [lax.rem(me + d, srcs) for d in range(1, srcs)]
    inner = list(range(1, planes - 1))
    edge = [0, planes - 1]
    slot = {p: p - 1 for p in inner}
    slot[0] = planes - 2
    slot[planes - 1] = planes - 1
    parts = ((0, planes - 2), (planes - 2, 1), (planes - 1, 1))

    loads = []
    for f in range(2):
        loads.append(pltpu.make_async_copy(
            fields.at[0, 2 * f], state.at[0, f, :, pl.ds(PAD, ny), :], load_sem.at[2 * f]))
        loads.append(pltpu.make_async_copy(fields.at[0, 2 * f + 1], prev.at[f], load_sem.at[2 * f + 1]))
    model_loads = [
        pltpu.make_async_copy(ref, models.at[m, :, pl.ds(PAD, ny), :], model_sem.at[m])
        for m, ref in enumerate((velocity, conductivity))
    ]
    for copy in loads + model_loads:
        copy.start()

    barrier = pltpu.get_barrier_semaphore()
    for exists, other in sides:
        @pl.when(exists)
        def _():
            pl.semaphore_signal(barrier, inc=1, device_id={"space": other}, device_id_type=MESH)
    for peer in peers:
        pl.semaphore_signal(barrier, inc=1, device_id={"src": peer}, device_id_type=MESH)

    weight = labels[0].astype(jnp.float32)
    label_own[...] = jnp.full(label_own.shape, weight, jnp.float32)
    lane = lax.broadcasted_iota(jnp.int32, (1, nz), 1)
    first_lane = lane == 0
    last_lane = lane == nz - 1
    zero_rows = jnp.zeros((PAD, nz), jnp.float32)
    for k in range(last):
        for f in range(2):
            for p in range(planes):
                state[k, f, p, pl.ds(0, PAD), :] = zero_rows
                state[k, f, p, pl.ds(PAD + ny, PAD), :] = zero_rows

    pl.semaphore_wait(barrier, srcs - 1 + has_low.astype(jnp.int32) + has_high.astype(jnp.int32))

    def halo_copy(k, f, side, i):
        plane = 0 if side == 0 else planes - 1
        if k == 0:
            source = fields.at[0, 2 * f, plane, pl.ds(i * piece, piece), :]
        else:
            source = state.at[k, f, plane, pl.ds(PAD + i * piece, piece), :]
        return pltpu.make_async_remote_copy(
            src_ref=source, dst_ref=halo.at[k, f, 1 - side, pl.ds(i * piece, piece), :],
            send_sem=halo_send.at[k, f, side, i], recv_sem=halo_recv.at[k, f, 1 - side, i],
            device_id={"space": sides[side][1]}, device_id_type=MESH)

    def halo_start(k, f):
        for i in range(PIECES):
            for side in range(2):
                @pl.when(sides[side][0])
                def _():
                    halo_copy(k, f, side, i).start()

    def halo_wait(k, f, side, i):
        @pl.when(sides[side][0])
        def _():
            ref = halo.at[k, f, side, pl.ds(i * piece, piece), :]
            pltpu.make_async_remote_copy(
                src_ref=ref, dst_ref=ref,
                send_sem=halo_send.at[k, f, side, i], recv_sem=halo_recv.at[k, f, side, i],
                device_id={"space": sides[side][1]}, device_id_type=MESH).wait_recv()

    def near_copy(m, side):
        ref = (velocity, conductivity)[m]
        plane = 0 if side == 0 else planes - 1
        return pltpu.make_async_remote_copy(
            src_ref=ref.at[plane, pl.ds(offset, band), :], dst_ref=near.at[m, 1 - side],
            send_sem=near_send.at[m, side], recv_sem=near_recv.at[m, 1 - side],
            device_id={"space": sides[side][1]}, device_id_type=MESH)

    def near_wait(m, side):
        pltpu.make_async_remote_copy(
            src_ref=near.at[m, side], dst_ref=near.at[m, side],
            send_sem=near_send.at[m, side], recv_sem=near_recv.at[m, side],
            device_id={"space": sides[side][1]}, device_id_type=MESH).wait_recv()

    def label_copy(d):
        return pltpu.make_async_remote_copy(
            src_ref=label_own, dst_ref=label_got.at[d],
            send_sem=label_send.at[d], recv_sem=label_recv.at[d],
            device_id={"src": peers[d]}, device_id_type=MESH)

    def grad_copy(part, d):
        begin, count = parts[part]
        return pltpu.make_async_remote_copy(
            src_ref=acc.at[pl.ds(begin, count), pl.ds(pl.multiple_of(peers[d] * band, 8), band), :],
            dst_ref=got.at[d, pl.ds(begin, count)],
            send_sem=grad_send.at[part, d], recv_sem=grad_recv.at[part, d],
            device_id={"src": peers[d]}, device_id_type=MESH)

    def fresh_copy(kind, part, d):
        begin, count = parts[part]
        return pltpu.make_async_remote_copy(
            src_ref=fresh.at[kind, d, pl.ds(begin, count)],
            dst_ref=updated.at[kind, pl.ds(begin, count), pl.ds(offset, band), :],
            send_sem=fresh_send.at[kind, part, d], recv_sem=fresh_recv.at[kind, part, d],
            device_id={"src": peers[d]}, device_id_type=MESH)

    def fresh_wait(kind, part, d):
        begin, count = parts[part]
        source = pl.multiple_of(lax.rem(me + srcs - 1 - d, srcs) * band, 8)
        ref = updated.at[kind, pl.ds(begin, count), pl.ds(source, band), :]
        pltpu.make_async_remote_copy(
            src_ref=ref, dst_ref=ref,
            send_sem=fresh_send.at[kind, part, d], recv_sem=fresh_recv.at[kind, part, d],
            device_id={"src": peers[d]}, device_id_type=MESH).wait_recv()

    halo_start(0, 0)
    halo_start(0, 1)
    for side in range(2):
        @pl.when(sides[side][0])
        def _():
            for m in range(2):
                near_copy(m, side).start()
    for d in range(srcs - 1):
        label_copy(d).start()

    for side in range(2):
        @pl.when(jnp.logical_not(sides[side][0]))
        def _():
            for k in range(last):
                for f in range(2):
                    halo[k, f, side] = jnp.zeros((ny, nz), jnp.float32)

    def in_rows(body, begin=0, count=ny):
        def step(i, carry):
            body(pl.multiple_of(begin + i * rows, 8))
            return carry
        lax.fori_loop(0, count // rows, step, 0, unroll=True)

    keep_gain = 1.0 + weight

    def advance(k, f, p, begin=0, count=ny):
        def body(r):
            def at(plane, shift):
                return state[k, f, plane, pl.ds(r + PAD + shift, rows), :]
            middle = at(p, 0)
            below = halo[k, f, 0, pl.ds(r, rows), :] if p == 0 else at(p - 1, 0)
            above = halo[k, f, 1, pl.ds(r, rows), :] if p == planes - 1 else at(p + 1, 0)
            total = below + above
            total = total + at(p, 1) + at(p, -1)
            right = jnp.where(last_lane, 0.0, pltpu.roll(middle, nz - 1, 1))
            left = jnp.where(first_lane, 0.0, pltpu.roll(middle, 1, 1))
            lap = total + right + left - 6.0 * middle
            if f == 0 and k < STEPS:
                term = state[k, 1, p, pl.ds(r + PAD, rows), :] * lap
                if k == 0:
                    acc[slot[p], pl.ds(r, rows), :] = term
                else:
                    acc[slot[p], pl.ds(r, rows), :] += term
            if k == 0:
                before = prev[f, p, pl.ds(r, rows), :]
            else:
                before = state[k - 1, f, p, pl.ds(r + PAD, rows), :]
            value = keep_gain * middle - weight * before + coef[slot[p], pl.ds(r, rows), :] * lap
            if k == last - 1:
                fields_out[0, f, p, pl.ds(r, rows), :] = value
            else:
                state[k + 1, f, p, pl.ds(r + PAD, rows), :] = value
        in_rows(body, begin, count)

    def form_coef(p, velocity_at, conductivity_at):
        def body(r):
            coef[slot[p], pl.ds(r, rows), :] = coefficient(weight, velocity_at(p, r), conductivity_at(p, r))
        in_rows(body)

    for copy in model_loads:
        copy.wait()
    for p in range(planes):
        form_coef(
            p,
            lambda p, r: models[0, p, pl.ds(r + PAD, rows), :],
            lambda p, r: models[1, p, pl.ds(r + PAD, rows), :],
        )
        for m in range(2):
            models[m, p, pl.ds(0, PAD), :] = jnp.broadcast_to(models[m, p, pl.ds(PAD, 1), :], (PAD, nz))
            models[m, p, pl.ds(PAD + ny, PAD), :] = jnp.broadcast_to(
                models[m, p, pl.ds(PAD + ny - 1, 1), :], (PAD, nz))
    for copy in loads:
        copy.wait()

    def boundary(k, f, then=None):
        for i in range(PIECES):
            for side in range(2):
                halo_wait(k, f, side, i)
                advance(k, f, edge[side], i * piece, piece)
                if k + 1 < last:
                    @pl.when(sides[side][0])
                    def _():
                        halo_copy(k + 1, f, side, i).start()
                if then is not None and i == PIECES - 1:
                    then(side)

    def interior(k, f):
        for p in inner:
            advance(k, f, p)

    def penalty():
        def prepare(p, carry):
            window[0, p] = models[0, p, pl.ds(offset, band + 2 * PAD), :]
            window[1, p] = jnp.log(models[1, p, pl.ds(offset, band + 2 * PAD), :])
            return carry
        for p in range(planes):
            prepare(p, 0)
        for side in range(2):
            @pl.when(sides[side][0])
            def _():
                for m in range(2):
                    near_wait(m, side)
                near[1, side] = jnp.log(near[1, side])

            @pl.when(jnp.logical_not(sides[side][0]))
            def _():
                for m in range(2):
                    near[m, side] = window[m, edge[side], pl.ds(PAD, band), :]
        for p in range(planes):
            diffs = []
            for m in range(2):
                middle = window[m, p, pl.ds(PAD, band), :]
                below = near[m, 0] if p == 0 else window[m, p - 1, pl.ds(PAD, band), :]
                above = near[m, 1] if p == planes - 1 else window[m, p + 1, pl.ds(PAD, band), :]
                dx = (above - below) * 0.5
                dy = (window[m, p, pl.ds(PAD + 1, band), :] - window[m, p, pl.ds(PAD - 1, band), :]) * 0.5
                right = jnp.where(last_lane, middle, pltpu.roll(middle, nz - 1, 1))
                left = jnp.where(first_lane, middle, pltpu.roll(middle, 1, 1))
                diffs.append((dx, dy, (right - left) * 0.5))
            (vx, vy, vz), (lx, ly, lz) = diffs
            cross_a = vy * lz - vz * ly
            cross_b = vz * lx - vx * lz
            cross_c = vx * ly - vy * lx
            pen[slot[p]] = penalty_gain * (cross_a * cross_a + cross_b * cross_b + cross_c * cross_c)

    scale = 1.0 / (20.0 * math.sqrt(groups))

    def renew(part):
        if part == 0:
            for d in range(srcs - 1):
                label_copy(d).wait_recv()
        for d in range(srcs - 1):
            grad_copy(part, d).wait_recv()
        begin, count = parts[part]
        for s in range(begin, begin + count):
            p = [q for q in slot if slot[q] == s][0]
            own = acc[s, pl.ds(offset, band), :]
            grad_v = weight * own
            grad_c = (1.0 - weight) * own
            for d in range(srcs - 1):
                theirs = got[d, s]
                label = label_got[d, pl.ds(0, 1), :]
                grad_v = grad_v + label * theirs
                grad_c = grad_c + (1.0 - label) * theirs
            new = []
            for m, grad in enumerate((grad_v, grad_c)):
                old = models[m, p, pl.ds(offset + PAD, band), :]
                new.append(old * jnp.exp(-step_size * jnp.tanh(scale * grad + pen[s])))
            for d in range(srcs):
                label = weight if d == srcs - 1 else label_got[srcs - 2 - d, pl.ds(0, 1), :]
                acoustic = jnp.broadcast_to(label, (band, nz)) > 0.5
                needed = jnp.where(acoustic, new[0], new[1])
                other = jnp.where(acoustic, new[1], new[0])
                if d == srcs - 1:
                    updated[0, s, pl.ds(offset, band), :] = needed
                    updated[1, s, pl.ds(offset, band), :] = other
                else:
                    fresh[0, d, s] = needed
                    fresh[1, d, s] = other
        for d in range(srcs - 1):
            fresh_copy(0, part, d).start()

    def take_models(part, chosen):
        for d in range(srcs - 1):
            fresh_wait(0, part, d)
        for p in chosen:
            form_coef(
                p,
                lambda p, r: updated[0, slot[p], pl.ds(r, rows), :],
                lambda p, r: updated[0, slot[p], pl.ds(r, rows), :],
            )

    def store_models():
        for part in range(3):
            for d in range(srcs - 1):
                fresh_wait(1, part, d)
        for p in range(planes):
            def body(r):
                needed = updated[0, slot[p], pl.ds(r, rows), :]
                other = updated[1, slot[p], pl.ds(r, rows), :]
                acoustic = jnp.full((rows, nz), weight) > 0.5
                models_out[0, p, pl.ds(r, rows), :] = jnp.where(acoustic, needed, other)
                models_out[1, p, pl.ds(r, rows), :] = jnp.where(acoustic, other, needed)
            in_rows(body)

    for k in range(STEPS - 1):
        interior(k, 0)
        interior(k, 1)
        if k == STEPS - 2:
            penalty()
        boundary(k, 0)
        boundary(k, 1)

    def send_grad(part):
        for d in range(srcs - 1):
            grad_copy(part, d).start()

    interior(STEPS - 1, 0)
    send_grad(0)
    interior(STEPS - 1, 1)
    boundary(STEPS - 1, 0, lambda side: send_grad(1 + side))
    renew(0)
    boundary(STEPS - 1, 1)
    renew(1)
    renew(2)
    take_models(0, inner)
    interior(STEPS, 0)
    interior(STEPS, 1)
    for side in range(2):
        take_models(1 + side, edge[side:side + 1])
    boundary(STEPS, 0)
    boundary(STEPS, 1)
    for part in range(3):
        for d in range(srcs - 1):
            fresh_copy(1, part, d).start()
    for k in range(STEPS + 1, last):
        interior(k, 0)
        interior(k, 1)
        if k == last - 1:
            store_models()
        boundary(k, 0)
        boundary(k, 1)

    for side in range(2):
        @pl.when(sides[side][0])
        def _():
            for m in range(2):
                near_copy(m, side).wait_send()
            for k in range(last):
                for f in range(2):
                    for i in range(PIECES):
                        halo_copy(k, f, side, i).wait_send()
    for d in range(srcs - 1):
        label_copy(d).wait_send()
        for part in range(3):
            grad_copy(part, d).wait_send()
            for kind in range(2):
                fresh_copy(kind, part, d).wait_send()


def shards(spaces, srcs, fields, velocity, conductivity, labels):
    planes, ny, nz = fields.shape[2:]
    band = ny // srcs
    last = 2 * STEPS
    groups = labels.shape[0] * srcs
    f32 = jnp.float32
    vmem = lambda *shape: pltpu.VMEM(shape, f32)
    dma = lambda *shape: pltpu.SemaphoreType.DMA(shape)
    anywhere = pl.BlockSpec(memory_space=pl.ANY)
    scratch = [
        vmem(last, 2, planes, ny + 2 * PAD, nz),
        vmem(2, planes, ny, nz),
        vmem(last, 2, 2, ny, nz),
        vmem(2, planes, ny + 2 * PAD, nz),
        vmem(2, 2, band, nz),
        vmem(2, planes, band + 2 * PAD, nz),
        vmem(planes, band, nz),
        vmem(planes, ny, nz),
        vmem(planes, ny, nz),
        vmem(srcs - 1, planes, band, nz),
        vmem(8, nz),
        vmem(srcs - 1, 8, nz),
        vmem(2, srcs - 1, planes, band, nz),
        vmem(2, planes, ny, nz),
        dma(4), dma(2),
        dma(last, 2, 2, PIECES), dma(last, 2, 2, PIECES), dma(2, 2), dma(2, 2),
        dma(srcs - 1), dma(srcs - 1), dma(3, srcs - 1), dma(3, srcs - 1),
        dma(2, 3, srcs - 1), dma(2, 3, srcs - 1),
    ]
    return tuple(pl.pallas_call(
        functools.partial(kernel, spaces, srcs, groups),
        out_shape=(
            pltpu.VMEM((1, 2, planes, ny, nz), f32),
            pltpu.VMEM((2, planes, ny, nz), f32),
        ),
        in_specs=[pl.BlockSpec(memory_space=pltpu.HBM)] * 3 + [pl.BlockSpec(memory_space=pltpu.SMEM)],
        out_specs=(pl.BlockSpec(memory_space=pltpu.VMEM),)*2,
        scratch_shapes=scratch,
        cost_estimate=pl.CostEstimate(
            flops=40 * last * 2 * planes * ny * nz, bytes_accessed=40 * planes * ny * nz, transcendentals=0),
        compiler_params=pltpu.CompilerParams(
            collective_id=0, has_side_effects=True, vmem_limit_bytes=56 * 1024 * 1024),
    )(fields, velocity, conductivity, labels))


def solution(mesh):
    in_specs = (
        P(("parts", "src"), None, "space", None, None),
        P(("parts", "space"), None, None),
        P(("parts", "space"), None, None),
        P(("parts", "src")),
    )
    out_specs = (
        P(("parts", "src"), None, "space", None, None),
        P(None, ("parts", "space"), None, None),
    )
    body = functools.partial(shards, mesh.shape["space"], mesh.shape["src"])
    return jax.shard_map(body, mesh=mesh, in_specs=in_specs, out_specs=out_specs, check_vma=False)
```

```python
import functools
import math

import jax
import jax.numpy as jnp
from jax import lax
from jax.experimental import pallas as pl
from jax.experimental.pallas import tpu as pltpu
from jax.sharding import PartitionSpec as P

STEPS = 3
PAD = 8
PIECES = 2
MESH = pl.DeviceIdType.MESH

speed_gain = 0.25
diffuse_gain = 0.15
step_size = 0.1
penalty_gain = 50.0


def coefficient(weight, velocity, conductivity):
    return weight * speed_gain * velocity**2 + (1.0 - weight) * diffuse_gain / conductivity


def kernel(
    spaces, srcs, groups,
    fields, velocity, conductivity, labels,
    fields_out, models_out,
    state, prev, halo, models, near, window, pen, coef, acc, got, label_own, label_got, fresh, updated,
    load_sem, model_sem,
    halo_send, halo_recv, near_send, near_recv,
    label_send, label_recv, grad_send, grad_recv, fresh_send, fresh_recv,
):
    planes, ny, nz = fields.shape[2:]
    band = ny // srcs
    piece = ny // PIECES
    rows = 32 if piece % 32 == 0 else 8
    last = 2 * STEPS
    tile = lax.axis_index("space")
    me = lax.axis_index("src")
    offset = pl.multiple_of(me * band, 8)
    has_low = tile > 0
    has_high = tile < spaces - 1
    sides = ((has_low, tile - 1), (has_high, tile + 1))
    peers = [lax.rem(me + d, srcs) for d in range(1, srcs)]
    inner = list(range(1, planes - 1))
    edge = [0, planes - 1]
    slot = {p: p - 1 for p in inner}
    slot[0] = planes - 2
    slot[planes - 1] = planes - 1
    parts = ((0, planes - 2), (planes - 2, 1), (planes - 1, 1))

    loads = []
    for f in range(2):
        loads.append(pltpu.make_async_copy(
            fields.at[0, 2 * f], state.at[0, f, :, pl.ds(PAD, ny), :], load_sem.at[2 * f]))
        loads.append(pltpu.make_async_copy(fields.at[0, 2 * f + 1], prev.at[f], load_sem.at[2 * f + 1]))
    model_loads = [
        pltpu.make_async_copy(ref, models.at[m, :, pl.ds(PAD, ny), :], model_sem.at[m])
        for m, ref in enumerate((velocity, conductivity))
    ]
    for copy in loads + model_loads:
        copy.start()

    barrier = pltpu.get_barrier_semaphore()
    for exists, other in sides:
        @pl.when(exists)
        def _():
            pl.semaphore_signal(barrier, inc=1, device_id={"space": other}, device_id_type=MESH)
    for peer in peers:
        pl.semaphore_signal(barrier, inc=1, device_id={"src": peer}, device_id_type=MESH)

    weight = labels[0].astype(jnp.float32)
    label_own[...] = jnp.full(label_own.shape, weight, jnp.float32)
    lane = lax.broadcasted_iota(jnp.int32, (1, nz), 1)
    first_lane = lane == 0
    last_lane = lane == nz - 1
    zero_rows = jnp.zeros((PAD, nz), jnp.float32)
    for k in range(last):
        for f in range(2):
            for p in range(planes):
                state[k, f, p, pl.ds(0, PAD), :] = zero_rows
                state[k, f, p, pl.ds(PAD + ny, PAD), :] = zero_rows

    pl.semaphore_wait(barrier, srcs - 1 + has_low.astype(jnp.int32) + has_high.astype(jnp.int32))

    def halo_copy(k, f, side, i):
        plane = 0 if side == 0 else planes - 1
        if k == 0:
            source = fields.at[0, 2 * f, plane, pl.ds(i * piece, piece), :]
        else:
            source = state.at[k, f, plane, pl.ds(PAD + i * piece, piece), :]
        return pltpu.make_async_remote_copy(
            src_ref=source, dst_ref=halo.at[k, f, 1 - side, pl.ds(i * piece, piece), :],
            send_sem=halo_send.at[k, f, side, i], recv_sem=halo_recv.at[k, f, 1 - side, i],
            device_id={"space": sides[side][1]}, device_id_type=MESH)

    def halo_start(k, f):
        for i in range(PIECES):
            for side in range(2):
                @pl.when(sides[side][0])
                def _():
                    halo_copy(k, f, side, i).start()

    def halo_wait(k, f, side, i):
        @pl.when(sides[side][0])
        def _():
            ref = halo.at[k, f, side, pl.ds(i * piece, piece), :]
            pltpu.make_async_remote_copy(
                src_ref=ref, dst_ref=ref,
                send_sem=halo_send.at[k, f, side, i], recv_sem=halo_recv.at[k, f, side, i],
                device_id={"space": sides[side][1]}, device_id_type=MESH).wait_recv()

    def near_copy(m, side):
        ref = (velocity, conductivity)[m]
        plane = 0 if side == 0 else planes - 1
        return pltpu.make_async_remote_copy(
            src_ref=ref.at[plane, pl.ds(offset, band), :], dst_ref=near.at[m, 1 - side],
            send_sem=near_send.at[m, side], recv_sem=near_recv.at[m, 1 - side],
            device_id={"space": sides[side][1]}, device_id_type=MESH)

    def near_wait(m, side):
        pltpu.make_async_remote_copy(
            src_ref=near.at[m, side], dst_ref=near.at[m, side],
            send_sem=near_send.at[m, side], recv_sem=near_recv.at[m, side],
            device_id={"space": sides[side][1]}, device_id_type=MESH).wait_recv()

    def label_copy(d):
        return pltpu.make_async_remote_copy(
            src_ref=label_own, dst_ref=label_got.at[d],
            send_sem=label_send.at[d], recv_sem=label_recv.at[d],
            device_id={"src": peers[d]}, device_id_type=MESH)

    def grad_copy(part, d):
        begin, count = parts[part]
        return pltpu.make_async_remote_copy(
            src_ref=acc.at[pl.ds(begin, count), pl.ds(pl.multiple_of(peers[d] * band, 8), band), :],
            dst_ref=got.at[d, pl.ds(begin, count)],
            send_sem=grad_send.at[part, d], recv_sem=grad_recv.at[part, d],
            device_id={"src": peers[d]}, device_id_type=MESH)

    def fresh_copy(kind, part, d):
        begin, count = parts[part]
        return pltpu.make_async_remote_copy(
            src_ref=fresh.at[kind, d, pl.ds(begin, count)],
            dst_ref=updated.at[kind, pl.ds(begin, count), pl.ds(offset, band), :],
            send_sem=fresh_send.at[kind, part, d], recv_sem=fresh_recv.at[kind, part, d],
            device_id={"src": peers[d]}, device_id_type=MESH)

    def fresh_wait(kind, part, d):
        begin, count = parts[part]
        source = pl.multiple_of(lax.rem(me + srcs - 1 - d, srcs) * band, 8)
        ref = updated.at[kind, pl.ds(begin, count), pl.ds(source, band), :]
        pltpu.make_async_remote_copy(
            src_ref=ref, dst_ref=ref,
            send_sem=fresh_send.at[kind, part, d], recv_sem=fresh_recv.at[kind, part, d],
            device_id={"src": peers[d]}, device_id_type=MESH).wait_recv()

    halo_start(0, 0)
    halo_start(0, 1)
    for side in range(2):
        @pl.when(sides[side][0])
        def _():
            for m in range(2):
                near_copy(m, side).start()
    for d in range(srcs - 1):
        label_copy(d).start()

    for side in range(2):
        @pl.when(jnp.logical_not(sides[side][0]))
        def _():
            for k in range(last):
                for f in range(2):
                    halo[k, f, side] = jnp.zeros((ny, nz), jnp.float32)

    def in_rows(body, begin=0, count=ny):
        def step(i, carry):
            body(pl.multiple_of(begin + i * rows, 8))
            return carry
        lax.fori_loop(0, count // rows, step, 0, unroll=True)

    keep_gain = 1.0 + weight

    def advance(k, f, p, begin=0, count=ny):
        def body(r):
            def at(plane, shift):
                return state[k, f, plane, pl.ds(r + PAD + shift, rows), :]
            middle = at(p, 0)
            below = halo[k, f, 0, pl.ds(r, rows), :] if p == 0 else at(p - 1, 0)
            above = halo[k, f, 1, pl.ds(r, rows), :] if p == planes - 1 else at(p + 1, 0)
            total = below + above
            total = total + at(p, 1) + at(p, -1)
            right = jnp.where(last_lane, 0.0, pltpu.roll(middle, nz - 1, 1))
            left = jnp.where(first_lane, 0.0, pltpu.roll(middle, 1, 1))
            lap = total + right + left - 6.0 * middle
            if f == 0 and k < STEPS:
                term = state[k, 1, p, pl.ds(r + PAD, rows), :] * lap
                if k == 0:
                    acc[slot[p], pl.ds(r, rows), :] = term
                else:
                    acc[slot[p], pl.ds(r, rows), :] += term
            if k == 0:
                before = prev[f, p, pl.ds(r, rows), :]
            else:
                before = state[k - 1, f, p, pl.ds(r + PAD, rows), :]
            value = keep_gain * middle - weight * before + coef[slot[p], pl.ds(r, rows), :] * lap
            if k == last - 1:
                fields_out[0, f, p, pl.ds(r, rows), :] = value
            else:
                state[k + 1, f, p, pl.ds(r + PAD, rows), :] = value
        in_rows(body, begin, count)

    def form_coef(p, velocity_at, conductivity_at):
        def body(r):
            coef[slot[p], pl.ds(r, rows), :] = coefficient(weight, velocity_at(p, r), conductivity_at(p, r))
        in_rows(body)

    for copy in model_loads:
        copy.wait()
    for p in range(planes):
        form_coef(
            p,
            lambda p, r: models[0, p, pl.ds(r + PAD, rows), :],
            lambda p, r: models[1, p, pl.ds(r + PAD, rows), :],
        )
        for m in range(2):
            models[m, p, pl.ds(0, PAD), :] = jnp.broadcast_to(models[m, p, pl.ds(PAD, 1), :], (PAD, nz))
            models[m, p, pl.ds(PAD + ny, PAD), :] = jnp.broadcast_to(
                models[m, p, pl.ds(PAD + ny - 1, 1), :], (PAD, nz))
    for copy in loads:
        copy.wait()

    def boundary(k, f, then=None):
        for i in range(PIECES):
            for side in range(2):
                halo_wait(k, f, side, i)
                advance(k, f, edge[side], i * piece, piece)
                if k + 1 < last:
                    @pl.when(sides[side][0])
                    def _():
                        halo_copy(k + 1, f, side, i).start()
                if then is not None and i == PIECES - 1:
                    then(side)

    def interior(k, f):
        for p in inner:
            advance(k, f, p)

    def penalty():
        def prepare(p, carry):
            window[0, p] = models[0, p, pl.ds(offset, band + 2 * PAD), :]
            window[1, p] = jnp.log(models[1, p, pl.ds(offset, band + 2 * PAD), :])
            return carry
        for p in range(planes):
            prepare(p, 0)
        for side in range(2):
            @pl.when(sides[side][0])
            def _():
                for m in range(2):
                    near_wait(m, side)
                near[1, side] = jnp.log(near[1, side])

            @pl.when(jnp.logical_not(sides[side][0]))
            def _():
                for m in range(2):
                    near[m, side] = window[m, edge[side], pl.ds(PAD, band), :]
        for p in range(planes):
            diffs = []
            for m in range(2):
                middle = window[m, p, pl.ds(PAD, band), :]
                below = near[m, 0] if p == 0 else window[m, p - 1, pl.ds(PAD, band), :]
                above = near[m, 1] if p == planes - 1 else window[m, p + 1, pl.ds(PAD, band), :]
                dx = (above - below) * 0.5
                dy = (window[m, p, pl.ds(PAD + 1, band), :] - window[m, p, pl.ds(PAD - 1, band), :]) * 0.5
                right = jnp.where(last_lane, middle, pltpu.roll(middle, nz - 1, 1))
                left = jnp.where(first_lane, middle, pltpu.roll(middle, 1, 1))
                diffs.append((dx, dy, (right - left) * 0.5))
            (vx, vy, vz), (lx, ly, lz) = diffs
            cross_a = vy * lz - vz * ly
            cross_b = vz * lx - vx * lz
            cross_c = vx * ly - vy * lx
            pen[slot[p]] = penalty_gain * (cross_a * cross_a + cross_b * cross_b + cross_c * cross_c)

    scale = 1.0 / (20.0 * math.sqrt(groups))

    def renew(part):
        if part == 0:
            for d in range(srcs - 1):
                label_copy(d).wait_recv()
        for d in range(srcs - 1):
            grad_copy(part, d).wait_recv()
        begin, count = parts[part]
        for s in range(begin, begin + count):
            p = [q for q in slot if slot[q] == s][0]
            own = acc[s, pl.ds(offset, band), :]
            grad_v = weight * own
            grad_c = (1.0 - weight) * own
            for d in range(srcs - 1):
                theirs = got[d, s]
                label = label_got[d, pl.ds(0, 1), :]
                grad_v = grad_v + label * theirs
                grad_c = grad_c + (1.0 - label) * theirs
            new = []
            for m, grad in enumerate((grad_v, grad_c)):
                old = models[m, p, pl.ds(offset + PAD, band), :]
                new.append(old * jnp.exp(-step_size * jnp.tanh(scale * grad + pen[s])))
            for d in range(srcs):
                label = weight if d == srcs - 1 else label_got[srcs - 2 - d, pl.ds(0, 1), :]
                acoustic = jnp.broadcast_to(label, (band, nz)) > 0.5
                needed = jnp.where(acoustic, new[0], new[1])
                other = jnp.where(acoustic, new[1], new[0])
                if d == srcs - 1:
                    updated[0, s, pl.ds(offset, band), :] = needed
                    updated[1, s, pl.ds(offset, band), :] = other
                else:
                    fresh[0, d, s] = needed
                    fresh[1, d, s] = other
        for d in range(srcs - 1):
            fresh_copy(0, part, d).start()

    def take_models(part, chosen):
        for d in range(srcs - 1):
            fresh_wait(0, part, d)
        for p in chosen:
            form_coef(
                p,
                lambda p, r: updated[0, slot[p], pl.ds(r, rows), :],
                lambda p, r: updated[0, slot[p], pl.ds(r, rows), :],
            )

    def store_models():
        for part in range(3):
            for d in range(srcs - 1):
                fresh_wait(1, part, d)
        for p in range(planes):
            def body(r):
                needed = updated[0, slot[p], pl.ds(r, rows), :]
                other = updated[1, slot[p], pl.ds(r, rows), :]
                acoustic = jnp.full((rows, nz), weight) > 0.5
                models_out[0, p, pl.ds(r, rows), :] = jnp.where(acoustic, needed, other)
                models_out[1, p, pl.ds(r, rows), :] = jnp.where(acoustic, other, needed)
            in_rows(body)

    def send_grad(part):
        for d in range(srcs - 1):
            grad_copy(part, d).start()

    interior(0, 0)
    for k in range(STEPS - 1):
        interior(k, 1)
        if k == STEPS - 2:
            penalty()
        boundary(k, 0)
        interior(k + 1, 0)
        if k == STEPS - 2:
            send_grad(0)
        boundary(k, 1)
    interior(STEPS - 1, 1)
    boundary(STEPS - 1, 0, lambda side: send_grad(1 + side))
    renew(0)
    boundary(STEPS - 1, 1)
    renew(1)
    renew(2)
    take_models(0, inner)
    interior(STEPS, 0)
    interior(STEPS, 1)
    for side in range(2):
        take_models(1 + side, edge[side:side + 1])
    boundary(STEPS, 0)
    boundary(STEPS, 1)
    for part in range(3):
        for d in range(srcs - 1):
            fresh_copy(1, part, d).start()
    for k in range(STEPS + 1, last):
        interior(k, 0)
        interior(k, 1)
        if k == last - 1:
            store_models()
        boundary(k, 0)
        boundary(k, 1)

    for side in range(2):
        @pl.when(sides[side][0])
        def _():
            for m in range(2):
                near_copy(m, side).wait_send()
            for k in range(last):
                for f in range(2):
                    for i in range(PIECES):
                        halo_copy(k, f, side, i).wait_send()
    for d in range(srcs - 1):
        label_copy(d).wait_send()
        for part in range(3):
            grad_copy(part, d).wait_send()
            for kind in range(2):
                fresh_copy(kind, part, d).wait_send()


def shards(spaces, srcs, fields, velocity, conductivity, labels):
    planes, ny, nz = fields.shape[2:]
    band = ny // srcs
    last = 2 * STEPS
    groups = labels.shape[0] * srcs
    f32 = jnp.float32
    vmem = lambda *shape: pltpu.VMEM(shape, f32)
    dma = lambda *shape: pltpu.SemaphoreType.DMA(shape)
    anywhere = pl.BlockSpec(memory_space=pl.ANY)
    scratch = [
        vmem(last, 2, planes, ny + 2 * PAD, nz),
        vmem(2, planes, ny, nz),
        vmem(last, 2, 2, ny, nz),
        vmem(2, planes, ny + 2 * PAD, nz),
        vmem(2, 2, band, nz),
        vmem(2, planes, band + 2 * PAD, nz),
        vmem(planes, band, nz),
        vmem(planes, ny, nz),
        vmem(planes, ny, nz),
        vmem(srcs - 1, planes, band, nz),
        vmem(8, nz),
        vmem(srcs - 1, 8, nz),
        vmem(2, srcs - 1, planes, band, nz),
        vmem(2, planes, ny, nz),
        dma(4), dma(2),
        dma(last, 2, 2, PIECES), dma(last, 2, 2, PIECES), dma(2, 2), dma(2, 2),
        dma(srcs - 1), dma(srcs - 1), dma(3, srcs - 1), dma(3, srcs - 1),
        dma(2, 3, srcs - 1), dma(2, 3, srcs - 1),
    ]
    return tuple(pl.pallas_call(
        functools.partial(kernel, spaces, srcs, groups),
        out_shape=(
            pltpu.VMEM((1, 2, planes, ny, nz), f32),
            pltpu.VMEM((2, planes, ny, nz), f32),
        ),
        in_specs=[pl.BlockSpec(memory_space=pltpu.HBM)] * 3 + [pl.BlockSpec(memory_space=pltpu.SMEM)],
        out_specs=(pl.BlockSpec(memory_space=pltpu.VMEM),)*2,
        scratch_shapes=scratch,
        cost_estimate=pl.CostEstimate(
            flops=40 * last * 2 * planes * ny * nz, bytes_accessed=40 * planes * ny * nz, transcendentals=0),
        compiler_params=pltpu.CompilerParams(
            collective_id=0, has_side_effects=True, vmem_limit_bytes=56 * 1024 * 1024),
    )(fields, velocity, conductivity, labels))


def solution(mesh):
    in_specs = (
        P(("parts", "src"), None, "space", None, None),
        P(("parts", "space"), None, None),
        P(("parts", "space"), None, None),
        P(("parts", "src")),
    )
    out_specs = (
        P(("parts", "src"), None, "space", None, None),
        P(None, ("parts", "space"), None, None),
    )
    body = functools.partial(shards, mesh.shape["space"], mesh.shape["src"])
    return jax.shard_map(body, mesh=mesh, in_specs=in_specs, out_specs=out_specs, check_vma=False)
```
